256 devices in a mesh: tensor: 4 (over x), expert: 32 (over y, z), dp: 2 (over core).
Axes of the slice: x: 4, y: 4, z: 8, core: 2. Of those that a mesh axis runs over, the one named last changes fastest.
Arguments:
- tokens: bfloat16 [16384, 2048], P(('expert', 'dp')), may hold values from -6 to 6
- grad_output: bfloat16 [16384, 2048], P(('expert', 'dp')), may hold values from -4 to 4
- gate_prob: float32 [16384], P(('expert', 'dp')), may hold values from 0.3 to 1
- expert_index: int32 [16384, 1], P(('expert', 'dp')), may hold values from 0 to 31, as said below
- slot_index: int32 [16384, 1], P(('expert', 'dp')), may hold values from 0 to 15, as said below
- up_weight: bfloat16 [32, 2048, 4096], P('expert', 'dp', 'tensor'), may hold values from -0.125 to 0.125
- down_weight: bfloat16 [32, 2048, 4096], P('expert', 'dp', 'tensor'), may hold values from -0.09375 to 0.09375
Outputs:
- grad_tokens: bfloat16 [16384, 2048], P(('expert', 'dp'), 'tensor')
- grad_up: bfloat16 [32, 2048, 4096], P('expert', 'dp', 'tensor')
- grad_down: bfloat16 [32, 2048, 4096], P('expert', 'dp', 'tensor')
The draws below stay inside these ranges and needn't reach their ends.
Inputs may be any that keep to these rules, and one draw needn't show every extreme that they name: `expert_index`: within each aligned block of 256 rows, at most 16 rows choose one expert; in every block one expert is chosen by exactly 16 rows, and other experts by varying numbers. `slot_index`: slots of rows that choose the same expert within an aligned block of 256 rows are distinct.
All inputs are finite; a program needn't handle non-finite values.
Results may differ from the reference program's by a relative error of at most 0.015.
Values may be sent and summed in bfloat16 or wider, within the bound.
A program may use at most 128 MiB of HBM per device.

```python
import jax
import jax.numpy as jnp
from jax import lax

D = 2048
H = 4096
TOP = 1
TOK_DEV = 256
EXPERTS = 32
CAP = 16
TOKENS = 16384
N_EXPERT = 32
N_DP = 2


def routing(key):
    busiest = jax.random.randint(jax.random.fold_in(key, 101), (), 0, EXPERTS).astype(jnp.int32)
    block_keys = jax.random.split(jax.random.fold_in(key, 102), TOKENS // TOK_DEV)
    pool = jnp.arange((EXPERTS - 1) * CAP, dtype=jnp.int32)
    own_slots = jnp.arange(CAP, dtype=jnp.int32)
    order = jnp.arange(TOK_DEV, dtype=jnp.int32)

    def per_block(block_key):
        first_key, second_key = jax.random.split(block_key)
        chosen = jax.random.permutation(first_key, pool)[:TOK_DEV - CAP]
        others = chosen // CAP
        others = (others + (others >= busiest).astype(jnp.int32)).astype(jnp.int32)
        expert_list = jnp.concatenate([jnp.zeros((CAP,), jnp.int32) + busiest, others])
        slot_list = jnp.concatenate([own_slots, (chosen % CAP).astype(jnp.int32)])
        shuffle = jax.random.permutation(second_key, order)
        return (expert_list[shuffle], slot_list[shuffle])
    expert_all, slot_all = jax.vmap(per_block)(block_keys)
    return (expert_all.reshape(TOKENS, TOP).astype(jnp.int32), slot_all.reshape(TOKENS, TOP).astype(jnp.int32))


def draw_expert_index(key, part):
    return routing(key)[0]


def draw_slot_index(key, part):
    return routing(key)[1]


def shard_levels(rng, shape, cuts, smallest, top_value):
    def one(position, parts):
        draws = jax.random.uniform(jax.random.fold_in(jax.random.fold_in(rng, 6), position), (parts,), jnp.float32, smallest / len(cuts), top_value / len(cuts))
        return jnp.repeat(jnp.exp(draws), shape[position] // parts).reshape((-1,) + (1,) * (len(shape) - position - 1))

    gain = one(*cuts[0])
    for cut in cuts[1:]:
        gain = gain * one(*cut)
    return gain


def scatter_about(own_key, shape, scale, bound, shards=(), kind=jnp.bfloat16):
    entries = jax.random.normal(own_key, shape, jnp.float32) * scale
    if len(shards) > 0:
        entries = shard_levels(own_key, shape, shards, -0.22, 0.18) * entries
    return jnp.clip(entries, min=-bound, max=bound).astype(kind)


def setup_inputs(seed: int = 0) -> dict:
    splits = jax.random.split(jax.random.key(seed), 8)
    return {
        "tokens": scatter_about(splits[0], (TOKENS, D), 1.0, 6.0, ((0, 64),)),
        "grad_output": scatter_about(splits[1], (TOKENS, D), 0.5, 4.0, ((0, 64),)),
        "gate_prob": jnp.clip(0.3 + 0.7 * jax.random.uniform(splits[2], (TOKENS,), jnp.float32) ** shard_levels(splits[2], (TOKENS,), ((0, 64),), -0.2, 0.2), 0.3, 1.0),
        "expert_index": draw_expert_index(jax.random.fold_in(splits[7], 71), 0),
        "slot_index": draw_slot_index(jax.random.fold_in(splits[7], 71), 0),
        "up_weight": scatter_about(splits[5], (EXPERTS, D, H), D ** -0.5, 0.125, ((0, 32), (1, 2), (2, 4))),
        "down_weight": scatter_about(splits[6], (EXPERTS, D, H), H ** -0.5, 0.09375, ((0, 32), (1, 2), (2, 4))),
    }


def expert_grads(token_rows, grad_rows, up_matrix, down_matrix):
    pre_act = jnp.dot(token_rows, up_matrix, preferred_element_type=jnp.float32)
    hidden = jax.nn.gelu(pre_act).astype(jnp.bfloat16)
    hidden_grad = jnp.dot(grad_rows, down_matrix, preferred_element_type=jnp.float32)
    slope_grad = jax.vjp(jax.nn.gelu, pre_act)[1](hidden_grad)[0].astype(jnp.bfloat16)
    input_part = lax.dot_general(slope_grad, up_matrix, (((1,), (1,)), ((), ())), preferred_element_type=jnp.float32)
    return (hidden, slope_grad, input_part)

def reference(tokens, grad_output, gate_prob, expert_index, slot_index, up_weight, down_weight):
    chosen_expert = expert_index[:, 0].astype(jnp.int32)
    chosen_slot = slot_index[:, 0].astype(jnp.int32)
    block_ids = jnp.arange(TOKENS, dtype=jnp.int32) // TOK_DEV
    source_rank = (block_ids // N_DP).astype(jnp.int32)
    replica = (block_ids % N_DP).astype(jnp.int32)
    scaled = (grad_output.astype(jnp.float32) * gate_prob[:, None]).astype(jnp.bfloat16)
    buf_shape = (EXPERTS, N_DP, N_EXPERT, CAP, D)
    token_buf = jnp.zeros(buf_shape, jnp.bfloat16).at[chosen_expert, replica, source_rank, chosen_slot].set(tokens)
    grad_buf = jnp.zeros(buf_shape, jnp.bfloat16).at[chosen_expert, replica, source_rank, chosen_slot].set(scaled)

    def per_expert(expert_items):
        token_part, grad_part, up_matrix, down_matrix = expert_items
        down_list = []
        up_list = []
        input_list = []
        for replica_id in range(N_DP):
            token_rows = token_part[replica_id].reshape(N_EXPERT * CAP, D)
            grad_rows = grad_part[replica_id].reshape(N_EXPERT * CAP, D)
            hidden, slope_grad, input_part = expert_grads(token_rows, grad_rows, up_matrix, down_matrix)
            down_term = jnp.dot(grad_rows.T, hidden, preferred_element_type=jnp.float32).astype(jnp.bfloat16)
            up_term = jnp.dot(token_rows.T, slope_grad, preferred_element_type=jnp.float32).astype(jnp.bfloat16)
            down_list.append(lax.optimization_barrier(down_term).astype(jnp.float32))
            up_list.append(lax.optimization_barrier(up_term).astype(jnp.float32))
            input_list.append(input_part.astype(jnp.bfloat16).reshape(N_EXPERT, CAP, D))
        return (sum(up_list).astype(jnp.bfloat16), sum(down_list).astype(jnp.bfloat16), jnp.stack(input_list))
    grad_up, grad_down, input_buf = lax.map(per_expert, (token_buf, grad_buf, up_weight, down_weight))
    grad_tokens = input_buf[chosen_expert, replica, source_rank, chosen_slot]
    return (grad_tokens, grad_up, grad_down)
```

```python
import jax
import jax.numpy as jnp
from jax import lax
from jax.experimental import pallas as pl
from jax.experimental.pallas import tpu as pltpu
from jax.sharding import PartitionSpec as P

MESH = pl.DeviceIdType.MESH
F32 = jnp.float32
BF16 = jnp.bfloat16
ROOT = 0.7978845608028654
CUBE = 0.044715

NY, NZ, NX = 4, 8, 4
CAP = 16
NS = NY * NZ
QUARTER = 512
PAIRS = 4


def dot(a, b, dims):
    return lax.dot_general(a, b, (dims, ((), ())), preferred_element_type=F32)


def activation(pre, back):
    square = pre * pre
    bent = jnp.tanh(ROOT * (pre + CUBE * (pre * square)))
    share = 0.5 * (1.0 + bent)
    slope = share + pre * (0.5 * (1.0 - bent * bent)) * (ROOT * (1.0 + 3.0 * CUBE * square))
    return (pre * share).astype(BF16), (back * slope).astype(BF16)


def kernel(
    pos_ref, gate_ref, tok_hbm, gout_hbm, up_hbm, down_hbm,
    ret, gu_out, gd_out,
    tokv, goutv, near, far, rows, prows, up, down, hs, phs, inp, ra, rb, rp, rm, res, gu, gd,
    load_sem, near_send, far_send, yz_recv, own_send, plus_recv, minus_recv, fwd_send, fplus_recv, fminus_recv,
    w_send, w_recv, dp_send, prow_recv, phs_recv,
    first_send, ra_recv, rb_recv, second_send, rp_recv, rm_recv, ret_send, ret_recv, out_sem,
):
    t = lax.axis_index("tensor")
    e = lax.axis_index("expert")
    d = lax.axis_index("dp")
    y, z = e // NZ, e % NZ
    left, right, across = (t + 3) % NX, (t + 1) % NX, (t + 2) % NX
    other = 1 - d

    def at_offset(s, sign):
        k, dy = s // NY, s % NY
        dz = ((k + 1) // 2) * (2 * (k % 2) - 1)
        return (t, ((y + sign * dy + NY) % NY) * NZ + (z + sign * dz + NZ) % NZ, d)

    right_dev, left_dev, other_dev = (right, e, d), (left, e, d), (t, e, other)

    def remote(src, dst, send, recv, dev):
        return pltpu.make_async_remote_copy(
            src_ref=src, dst_ref=dst, send_sem=send, recv_sem=recv, device_id=dev, device_id_type=MESH
        )

    loads = [
        pltpu.make_async_copy(tok_hbm, tokv, load_sem.at[0]),
        pltpu.make_async_copy(gout_hbm, goutv, load_sem.at[1]),
        pltpu.make_async_copy(up_hbm, up.at[pl.ds(d * 1024, 1024)], load_sem.at[2]),
        pltpu.make_async_copy(down_hbm, down.at[pl.ds(d * 1024, 1024)], load_sem.at[3]),
    ]
    for copy in loads:
        copy.start()

    barrier = pltpu.get_barrier_semaphore()

    def greet(s, _):
        pl.semaphore_signal(barrier, inc=1, device_id=at_offset(s, 1), device_id_type=MESH)
        return 0

    for dev in (right_dev, left_dev, other_dev):
        pl.semaphore_signal(barrier, inc=1, device_id=dev, device_id_type=MESH)
    lax.fori_loop(1, NS, greet, 0)

    pos = pos_ref[...]
    gate = gate_ref[...]
    hot_near = lax.broadcasted_iota(jnp.int32, (NY * CAP, pos.shape[1]), 0) == pos
    hot_far = lax.broadcasted_iota(jnp.int32, ((NS - NY) * CAP, pos.shape[1]), 0) + NY * CAP == pos
    gate_near = jnp.sum(jnp.where(hot_near, gate, 0.0), axis=1, keepdims=True)
    gate_far = jnp.sum(jnp.where(hot_far, gate, 0.0), axis=1, keepdims=True)
    hot_near = hot_near.astype(BF16)
    hot_far = hot_far.astype(BF16)
    mine = pl.ds(pl.multiple_of(t * QUARTER, QUARTER), QUARTER)
    for part, buf in ((0, tokv), (1, goutv)):
        loads[part].wait()
        for q in range(4):
            placed = dot(hot_near, buf[:, q * QUARTER:(q + 1) * QUARTER], ((1,), (0,)))
            if part == 1:
                placed = placed * gate_near
            placed = placed.astype(BF16).reshape(NY, CAP, QUARTER)
            near[q, :, part] = placed
            rows[q, 0, part] = placed[0]
        placed = dot(hot_far, buf[:, mine], ((1,), (0,)))
        if part == 1:
            placed = placed * gate_far
        far[:, part] = placed.astype(BF16).reshape(NS - NY, CAP, QUARTER)

    pl.semaphore_wait(barrier, NS - 1 + 3)

    def send_near(s, _):
        remote(near.at[:, s], rows.at[:, s], near_send, yz_recv.at[0], at_offset(s, 1)).start()
        return 0

    def send_far(s, _):
        remote(far.at[s - NY], rows.at[t, s], far_send, yz_recv.at[s // NY], at_offset(s, 1)).start()
        return 0

    weights = []
    for i, (src, dst) in enumerate(((up_hbm, up), (down_hbm, down))):
        weights.append(remote(src, dst.at[pl.ds(d * 1024, 1024)], w_send.at[i], w_recv.at[i], other_dev))
    lax.fori_loop(1, NY, send_near, 0)
    lax.fori_loop(NY, NS, send_far, 0)
    for copy in weights:
        copy.start()

    def block(q, k, n=NY, skip=0):
        return rows.at[q, pl.ds(NY * k + skip, n)]

    def gather_own(k):
        mine = block(t, k)
        remote(mine, mine, far_send, yz_recv.at[k], left_dev).wait_recv()
        remote(mine, mine, own_send.at[0], plus_recv.at[k], right_dev).start()
        remote(mine, mine, own_send.at[1], minus_recv.at[k], left_dev).start()

    def gather_pass(k):
        got = block(left, k)
        remote(got, got, own_send.at[0], plus_recv.at[k], right_dev).wait_recv()
        half = block(left, k, 2)
        remote(half, half, fwd_send.at[0], fplus_recv.at[k], right_dev).start()
        got = block(right, k)
        remote(got, got, own_send.at[1], minus_recv.at[k], left_dev).wait_recv()
        half = block(right, k, 2, 2)
        remote(half, half, fwd_send.at[1], fminus_recv.at[k], left_dev).start()

    def gather_end(k):
        half = block(across, k, 2)
        remote(half, half, fwd_send.at[0], fplus_recv.at[k], right_dev).wait_recv()
        half = block(across, k, 2, 2)
        remote(half, half, fwd_send.at[1], fminus_recv.at[k], left_dev).wait_recv()

    def near_end():
        got = rows.at[:, pl.ds(1, NY - 1)]
        remote(got, got, near_send, yz_recv.at[0], left_dev).wait_recv()

    def products(p):
        part = pl.ds(8 * p, 8)
        span = pl.ds(128 * p, 128)
        remote(
            rows.at[pl.ds(2 * other, 2), part], prows.at[:, part], dp_send.at[0], prow_recv, other_dev
        ).start()
        for c in range(0, 1024, 256):
            cols = pl.ds(c, 256)
            pre = jnp.zeros((128, 256), F32)
            back = jnp.zeros((128, 256), F32)
            for q in range(4):
                depth = pl.ds(q * QUARTER, QUARTER)
                pre += dot(rows[q, part, 0].reshape(128, QUARTER), up[depth, cols], ((1,), (0,)))
                back += dot(rows[q, part, 1].reshape(128, QUARTER), down[depth, cols], ((1,), (0,)))
            hidden, slope = activation(pre, back)
            hs[0, span, cols] = hidden
            hs[1, span, cols] = slope
        remote(hs.at[:, span], phs.at[:, span], dp_send.at[1], phs_recv, other_dev).start()

    def input_share(p, q):
        span = pl.ds(128 * p, 128)
        depth = pl.ds(pl.multiple_of(q * QUARTER, QUARTER), QUARTER)
        inp[p, q] = dot(hs[1, span, :], up[depth, :], ((1,), (1,))).astype(BF16)

    def sum_first(p):
        input_share(p, across)
        remote(
            inp.at[p, across, pl.ds(0, 64)], ra.at[p], first_send.at[0], ra_recv.at[p], right_dev
        ).start()
        remote(
            inp.at[p, across, pl.ds(64, 64)], rb.at[p], first_send.at[1], rb_recv.at[p], left_dev
        ).start()
        input_share(p, right)
        input_share(p, left)
        input_share(p, t)

    def sum_second(p):
        remote(ra.at[p], ra.at[p], first_send.at[0], ra_recv.at[p], right_dev).wait_recv()
        top = pl.ds(0, 64)
        inp[p, right, top] = (inp[p, right, top].astype(F32) + ra[p].astype(F32)).astype(BF16)
        remote(inp.at[p, right], rp.at[p], second_send.at[0], rp_recv.at[p], right_dev).start()
        remote(rb.at[p], rb.at[p], first_send.at[1], rb_recv.at[p], left_dev).wait_recv()
        low = pl.ds(64, 64)
        inp[p, left, low] = (inp[p, left, low].astype(F32) + rb[p].astype(F32)).astype(BF16)
        remote(inp.at[p, left], rm.at[p], second_send.at[1], rm_recv.at[p], left_dev).start()

    def sum_last(p):
        remote(rp.at[p], rp.at[p], second_send.at[0], rp_recv.at[p], right_dev).wait_recv()
        remote(rm.at[p], rm.at[p], second_send.at[1], rm_recv.at[p], left_dev).wait_recv()
        total = inp[p, t].astype(F32) + rp[p].astype(F32) + rm[p].astype(F32)
        res[pl.ds(8 * p, 8)] = total.astype(BF16).reshape(8, CAP, QUARTER)

        def give_back(s, _):
            remote(res.at[s], ret.at[s], ret_send, ret_recv, at_offset(s, -1)).start()
            return 0

        lax.fori_loop(max(8 * p, 1), 8 * p + 8, give_back, 0)

    def weight_grads(which, q):
        out = gu if which == 0 else gd
        a = rows[2 * d + q, :, which].reshape(NS * CAP, QUARTER)
        b = prows[q, :, which].reshape(NS * CAP, QUARTER)
        for c in range(0, 1024, 256):
            cols = pl.ds(c, 256)
            total = dot(a, hs[1 - which, :, cols], ((0,), (0,)))
            total += dot(b, phs[1 - which, :, cols], ((0,), (0,)))
            out[pl.ds(q * QUARTER, QUARTER), cols] = total.astype(BF16)

    gather_own(1)
    for copy in loads[2:]:
        copy.wait()
    gather_own(2)
    gather_pass(1)
    for copy in weights:
        copy.wait_recv()
    near_end()
    gather_own(3)
    gather_pass(2)
    gather_end(1)
    products(0)
    sum_first(0)
    gather_own(4)
    gather_pass(3)
    gather_end(2)
    gather_end(3)
    products(1)
    sum_first(1)
    sum_second(0)
    gather_own(5)
    gather_pass(4)
    sum_second(1)
    sum_last(0)
    gather_own(6)
    gather_pass(5)
    gather_end(4)
    gather_end(5)
    products(2)
    sum_first(2)
    sum_last(1)
    gather_own(7)
    gather_pass(6)
    sum_second(2)
    gather_pass(7)
    sum_last(2)
    gather_end(6)
    gather_end(7)
    products(3)
    sum_first(3)
    remote(
        rows.at[pl.ds(0, 2)], prows, dp_send.at[0], prow_recv, other_dev
    ).wait_recv()
    remote(hs, phs, dp_send.at[1], phs_recv, other_dev).wait_recv()
    weight_grads(0, 0)
    sum_second(3)
    weight_grads(0, 1)
    copy_up = pltpu.make_async_copy(gu, gu_out, out_sem.at[0])
    copy_up.start()
    sum_last(3)
    weight_grads(1, 0)
    weight_grads(1, 1)
    copy_down = pltpu.make_async_copy(gd, gd_out, out_sem.at[1])
    copy_down.start()
    copy_own = pltpu.make_async_copy(res.at[0], ret.at[0], out_sem.at[2])
    copy_own.start()

    got = ret.at[pl.ds(1, NS - 1)]
    sent = res.at[pl.ds(1, NS - 1)]
    remote(sent, got, ret_send, ret_recv, left_dev).wait()
    remote(near.at[:, pl.ds(1, NY - 1)], rows.at[:, pl.ds(1, NY - 1)], near_send, yz_recv.at[0], left_dev).wait_send()
    remote(far, far, far_send, yz_recv.at[0], left_dev).wait_send()
    for i in range(2):
        own = rows.at[0, pl.ds(NY, NS - NY)]
        half = rows.at[0, pl.ds(NY, (NS - NY) // 2)]
        remote(own, own, own_send.at[i], plus_recv.at[0], left_dev).wait_send()
        remote(half, half, fwd_send.at[i], plus_recv.at[0], left_dev).wait_send()
        weights[i].wait_send()
        remote(ra, ra, first_send.at[i], ra_recv.at[0], left_dev).wait_send()
        remote(rp, rp, second_send.at[i], rp_recv.at[0], left_dev).wait_send()
    remote(prows, prows, dp_send.at[0], prow_recv, other_dev).wait_send()
    remote(hs, phs, dp_send.at[1], phs_recv, other_dev).wait_send()
    copy_up.wait()
    copy_down.wait()
    copy_own.wait()


def local(tokens, grad_output, gate_prob, expert_index, slot_index, up_weight, down_weight):
    count = tokens.shape[0]
    e = lax.axis_index("expert")
    y, z = e // NZ, e % NZ
    chosen = expert_index[:, 0]
    dy = (chosen // NZ - y + NY) % NY
    dz = (chosen % NZ - z + NZ) % NZ
    k = jnp.where(dz > NZ // 2, 2 * (NZ - dz), jnp.maximum(2 * dz - 1, 0))
    pos = (NY * k + dy) * CAP + slot_index[:, 0]
    vmem = pl.BlockSpec(memory_space=pltpu.VMEM)
    hbm = pl.BlockSpec(memory_space=pl.ANY)
    dma = pltpu.SemaphoreType.DMA
    shape = jax.ShapeDtypeStruct
    returned, grad_up, grad_down = pl.pallas_call(
        kernel,
        out_shape=(
            shape((NS, CAP, QUARTER), BF16),
            shape((1024, 1024), BF16),
            shape((1024, 1024), BF16),
        ),
        in_specs=[vmem, vmem, hbm, hbm, hbm, hbm],
        out_specs=(hbm, hbm, hbm),
        scratch_shapes=[
            pltpu.VMEM((count, 2048), BF16),
            pltpu.VMEM((count, 2048), BF16),
            pltpu.VMEM((4, NY, 2, CAP, QUARTER), BF16),
            pltpu.VMEM((NS - NY, 2, CAP, QUARTER), BF16),
            pltpu.VMEM((4, NS, 2, CAP, QUARTER), BF16),
            pltpu.VMEM((2, NS, 2, CAP, QUARTER), BF16),
            pltpu.VMEM((2048, 1024), BF16),
            pltpu.VMEM((2048, 1024), BF16),
            pltpu.VMEM((2, 512, 1024), BF16),
            pltpu.VMEM((2, 512, 1024), BF16),
            pltpu.VMEM((PAIRS, 4, 128, QUARTER), BF16),
            pltpu.VMEM((PAIRS, 64, QUARTER), BF16),
            pltpu.VMEM((PAIRS, 64, QUARTER), BF16),
            pltpu.VMEM((PAIRS, 128, QUARTER), BF16),
            pltpu.VMEM((PAIRS, 128, QUARTER), BF16),
            pltpu.VMEM((NS, CAP, QUARTER), BF16),
            pltpu.VMEM((1024, 1024), BF16),
            pltpu.VMEM((1024, 1024), BF16),
            dma((4,)), dma, dma, dma((NZ,)), dma((2,)), dma((NZ,)), dma((NZ,)), dma((2,)), dma((NZ,)), dma((NZ,)),
            dma((2,)), dma((2,)), dma((2,)), dma, dma,
            dma((2,)), dma((PAIRS,)), dma((PAIRS,)), dma((2,)), dma((PAIRS,)), dma((PAIRS,)), dma, dma, dma((3,)),
        ],
        compiler_params=pltpu.CompilerParams(
            collective_id=0, has_side_effects=True, vmem_limit_bytes=48 * 2**20
        ),
        cost_estimate=pl.CostEstimate(flops=11 * 10**9, bytes_accessed=12 * 2**20, transcendentals=2**19),
        name="expert_layer",
    )(pos[None, :], gate_prob[None, :], tokens, grad_output, up_weight[0], down_weight[0])
    onehot = (lax.broadcasted_iota(jnp.int32, (NS * CAP, count), 0) == pos[None, :]).astype(BF16)
    grad_tokens = dot(onehot, returned.reshape(NS * CAP, QUARTER), ((0,), (0,)))
    return grad_tokens.astype(BF16), grad_up[None], grad_down[None]


def solution(mesh):
    placed = (
        P(("expert", "dp"), None),
        P(("expert", "dp"), None),
        P(("expert", "dp")),
        P(("expert", "dp"), None),
        P(("expert", "dp"), None),
        P("expert", "dp", "tensor"),
        P("expert", "dp", "tensor"),
    )
    return jax.shard_map(
        local,
        mesh=mesh,
        in_specs=placed,
        out_specs=(
            P(("expert", "dp"), "tensor"),
            P("expert", "dp", "tensor"),
            P("expert", "dp", "tensor"),
        ),
        check_vma=False,
    )
```

```python
import jax
import jax.numpy as jnp
from jax import lax
from jax.experimental import pallas as pl
from jax.experimental.pallas import tpu as pltpu
from jax.sharding import PartitionSpec as P

MESH = pl.DeviceIdType.MESH
F32 = jnp.float32
BF16 = jnp.bfloat16
ROOT = 0.7978845608028654
CUBE = 0.044715

NY, NZ, NX = 4, 8, 4
CAP = 16
NS = NY * NZ
QUARTER = 512
PAIRS = 4
OFFSETS = (
    (0, 0), (1, 0), (3, 0), (2, 0),
    (0, 1), (0, -1), (1, 1), (3, -1),
    (2, 1), (2, -1), (3, 1), (1, -1),
    (0, 2), (0, -2), (1, 2), (1, -2),
    (2, 2), (2, -2), (3, 2), (3, -2),
    (0, 3), (0, -3), (1, 3), (1, -3),
    (2, 3), (2, -3), (3, 3), (3, -3),
    (0, 4), (1, 4), (2, 4), (3, 4),
)
NEAR = 8
SEND_ORDER = (2, 0, 1, 3, 4, 5, 6, 7)


def positions(expert, slot):
    e = lax.axis_index("expert")
    y, z = e // NZ, e % NZ
    code = (((expert >> 3) - y) & (NY - 1)) * NZ + (((expert & (NZ - 1)) - z) & (NZ - 1))
    place = jnp.zeros_like(code)
    for s, (dy, dz) in enumerate(OFFSETS):
        place = place + jnp.where(code == dy * NZ + dz % NZ, s, 0)
    return place * CAP + slot


def dot(a, b, dims):
    return lax.dot_general(a, b, (dims, ((), ())), preferred_element_type=F32)


def activation(pre, back):
    square = pre * pre
    bent = jnp.tanh(ROOT * (pre + CUBE * (pre * square)))
    share = 0.5 * (1.0 + bent)
    slope = share + pre * (0.5 * (1.0 - bent * bent)) * (ROOT * (1.0 + 3.0 * CUBE * square))
    return (pre * share).astype(BF16), (back * slope).astype(BF16)


def kernel(
    expert_hbm, slot_hbm, gate_hbm, tok_hbm, gout_hbm, up_hbm, down_hbm,
    ret, gu, gd,
    expert_ref, slot_ref, gate_ref, tokv, goutv, near, far, rows, prows, up, down, hs, phs, inp, ra, rb, rp, rm, res, gsum,
    load_sem, small_sem, near_send, far_send, yz_recv, own_send, plus_recv, minus_recv, fwd_send, fplus_recv, fminus_recv,
    w_send, w_recv, dp_send, prow_recv, phs_recv,
    first_send, ra_recv, rb_recv, second_send, rp_recv, rm_recv, ret_send, ret_recv,
):
    t = lax.axis_index("tensor")
    e = lax.axis_index("expert")
    d = lax.axis_index("dp")
    y, z = e // NZ, e % NZ
    left, right, across = (t + 3) % NX, (t + 1) % NX, (t + 2) % NX
    other = 1 - d

    def at_offset(s, sign):
        dy, dz = OFFSETS[s]
        return (t, ((y + sign * dy + NY) % NY) * NZ + (z + sign * dz + NZ) % NZ, d)

    right_dev, left_dev, other_dev = (right, e, d), (left, e, d), (t, e, other)

    def remote(src, dst, send, recv, dev):
        return pltpu.make_async_remote_copy(
            src_ref=src, dst_ref=dst, send_sem=send, recv_sem=recv, device_id=dev, device_id_type=MESH
        )

    loads = [
        pltpu.make_async_copy(tok_hbm, tokv, load_sem.at[0]),
        pltpu.make_async_copy(gout_hbm, goutv, load_sem.at[1]),
        pltpu.make_async_copy(up_hbm, up.at[pl.ds(d * 1024, 1024)], load_sem.at[2]),
        pltpu.make_async_copy(down_hbm, down.at[pl.ds(d * 1024, 1024)], load_sem.at[3]),
    ]
    small = [
        pltpu.make_async_copy(src, dst, small_sem.at[i])
        for i, (src, dst) in enumerate(((expert_hbm, expert_ref), (slot_hbm, slot_ref), (gate_hbm, gate_ref)))
    ]
    for copy in small + loads:
        copy.start()

    barrier = pltpu.get_barrier_semaphore()

    for dev in (right_dev, left_dev, other_dev):
        pl.semaphore_signal(barrier, inc=1, device_id=dev, device_id_type=MESH)
    for s in range(1, NS):
        pl.semaphore_signal(barrier, inc=1, device_id=at_offset(s, 1), device_id_type=MESH)

    for copy in small:
        copy.wait()
    pos = positions(expert_ref[...], slot_ref[...])
    gate = gate_ref[...]
    hot_near = lax.broadcasted_iota(jnp.int32, (NEAR * CAP, pos.shape[1]), 0) == pos
    hot_far = lax.broadcasted_iota(jnp.int32, ((NS - NEAR) * CAP, pos.shape[1]), 0) + NEAR * CAP == pos
    gate_near = jnp.sum(jnp.where(hot_near, gate, 0.0), axis=1, keepdims=True)
    gate_far = jnp.sum(jnp.where(hot_far, gate, 0.0), axis=1, keepdims=True)
    hot_near = hot_near.astype(BF16)
    hot_far = hot_far.astype(BF16)
    mine = pl.ds(pl.multiple_of(t * QUARTER, QUARTER), QUARTER)
    for part, buf in ((0, tokv), (1, goutv)):
        loads[part].wait()
        placed = dot(hot_far, buf[:, mine], ((1,), (0,)))
        if part == 1:
            placed = placed * gate_far
        far[:, part] = placed.astype(BF16).reshape(NS - NEAR, CAP, QUARTER)
        for q in range(4):
            placed = dot(hot_near, buf[:, q * QUARTER:(q + 1) * QUARTER], ((1,), (0,)))
            if part == 1:
                placed = placed * gate_near
            placed = placed.astype(BF16).reshape(NEAR, CAP, QUARTER)
            near[q, :, part] = placed
            rows[q, 0, part] = placed[0]

    pl.semaphore_wait(barrier, NS - 1 + 3)

    for g in SEND_ORDER:
        for s in range(max(4 * g, 1), 4 * g + 4):
            if s < NEAR:
                remote(near.at[:, s], rows.at[:, s], near_send, yz_recv.at[g], at_offset(s, 1)).start()
            else:
                remote(far.at[s - NEAR], rows.at[t, s], far_send, yz_recv.at[g], at_offset(s, 1)).start()
    weights = []
    for i, (src, dst) in enumerate(((up_hbm, up), (down_hbm, down))):
        weights.append(remote(src, dst.at[pl.ds(d * 1024, 1024)], w_send.at[i], w_recv.at[i], other_dev))
        weights[i].start()

    def block(q, k, n=NY, skip=0):
        return rows.at[q, pl.ds(NY * k + skip, n)]

    def gather_own(k):
        mine = block(t, k)
        remote(mine, mine, far_send, yz_recv.at[k], left_dev).wait_recv()
        remote(mine, mine, own_send.at[0], plus_recv.at[k], right_dev).start()
        remote(mine, mine, own_send.at[1], minus_recv.at[k], left_dev).start()

    def gather_pass(k):
        got = block(left, k)
        remote(got, got, own_send.at[0], plus_recv.at[k], right_dev).wait_recv()
        half = block(left, k, 2)
        remote(half, half, fwd_send.at[0], fplus_recv.at[k], right_dev).start()
        got = block(right, k)
        remote(got, got, own_send.at[1], minus_recv.at[k], left_dev).wait_recv()
        half = block(right, k, 2, 2)
        remote(half, half, fwd_send.at[1], fminus_recv.at[k], left_dev).start()

    def gather_end(k):
        half = block(across, k, 2)
        remote(half, half, fwd_send.at[0], fplus_recv.at[k], right_dev).wait_recv()
        half = block(across, k, 2, 2)
        remote(half, half, fwd_send.at[1], fminus_recv.at[k], left_dev).wait_recv()

    def near_end(g):
        got = rows.at[:, pl.ds(max(4 * g, 1), 4 * g + 4 - max(4 * g, 1))]
        remote(got, got, near_send, yz_recv.at[g], left_dev).wait_recv()

    def products(p, c):
        part = pl.ds(8 * p, 8)
        span = pl.ds(128 * p, 128)
        if c == 0:
            remote(
                rows.at[pl.ds(2 * other, 2), part], prows.at[:, part], dp_send.at[0], prow_recv.at[p], other_dev
            ).start()
        cols = pl.ds(256 * c, 256)
        pre = jnp.zeros((128, 256), F32)
        back = jnp.zeros((128, 256), F32)
        for q in range(4):
            depth = pl.ds(q * QUARTER, QUARTER)
            pre += dot(rows[q, part, 0].reshape(128, QUARTER), up[depth, cols], ((1,), (0,)))
            back += dot(rows[q, part, 1].reshape(128, QUARTER), down[depth, cols], ((1,), (0,)))
        hidden, slope = activation(pre, back)
        hs[0, span, cols] = hidden
        hs[1, span, cols] = slope
        if c == 3:
            remote(hs.at[:, span], phs.at[:, span], dp_send.at[1], phs_recv.at[p], other_dev).start()

    def input_share(p, q):
        span = pl.ds(128 * p, 128)
        depth = pl.ds(pl.multiple_of(q * QUARTER, QUARTER), QUARTER)
        inp[p, q] = dot(hs[1, span, :], up[depth, :], ((1,), (1,))).astype(BF16)

    def sum_first(p):
        input_share(p, across)
        remote(
            inp.at[p, across, pl.ds(0, 64)], ra.at[p], first_send.at[0], ra_recv.at[p], right_dev
        ).start()
        remote(
            inp.at[p, across, pl.ds(64, 64)], rb.at[p], first_send.at[1], rb_recv.at[p], left_dev
        ).start()
        input_share(p, right)
        input_share(p, left)
        input_share(p, t)

    def sum_second(p):
        remote(ra.at[p], ra.at[p], first_send.at[0], ra_recv.at[p], right_dev).wait_recv()
        top = pl.ds(0, 64)
        inp[p, right, top] = (inp[p, right, top].astype(F32) + ra[p].astype(F32)).astype(BF16)
        remote(inp.at[p, right], rp.at[p], second_send.at[0], rp_recv.at[p], right_dev).start()
        remote(rb.at[p], rb.at[p], first_send.at[1], rb_recv.at[p], left_dev).wait_recv()
        low = pl.ds(64, 64)
        inp[p, left, low] = (inp[p, left, low].astype(F32) + rb[p].astype(F32)).astype(BF16)
        remote(inp.at[p, left], rm.at[p], second_send.at[1], rm_recv.at[p], left_dev).start()

    def sum_last(p):
        remote(rp.at[p], rp.at[p], second_send.at[0], rp_recv.at[p], right_dev).wait_recv()
        remote(rm.at[p], rm.at[p], second_send.at[1], rm_recv.at[p], left_dev).wait_recv()
        total = inp[p, t].astype(F32) + rp[p].astype(F32) + rm[p].astype(F32)
        res[pl.ds(8 * p, 8)] = total.astype(BF16).reshape(8, CAP, QUARTER)

        if p == 0:
            ret[0] = total[:CAP].astype(BF16)
        for s in range(max(8 * p, 1), 8 * p + 8):
            remote(res.at[s], ret.at[s], ret_send, ret_recv, at_offset(s, -1)).start()

    def partner_rows(p):
        part = pl.ds(8 * p, 8)
        span = pl.ds(128 * p, 128)
        remote(
            rows.at[pl.ds(0, 2), part], prows.at[:, part], dp_send.at[0], prow_recv.at[p], other_dev
        ).wait_recv()
        remote(hs.at[:, span], phs.at[:, span], dp_send.at[1], phs_recv.at[p], other_dev).wait_recv()

    def weight_grads(half, which, q):
        out = gu if which == 0 else gd
        part = pl.ds(16 * half, 16)
        span = pl.ds(256 * half, 256)
        where = pl.ds(q * QUARTER, QUARTER)
        a = rows[2 * d + q, part, which].reshape(256, QUARTER)
        b = prows[q, part, which].reshape(256, QUARTER)
        for c in range(0, 1024, 256):
            cols = pl.ds(c, 256)
            total = dot(a, hs[1 - which, span, cols], ((0,), (0,)))
            total += dot(b, phs[1 - which, span, cols], ((0,), (0,)))
            if half == 0:
                gsum[which, where, cols] = total
            else:
                out[where, cols] = (gsum[which, where, cols] + total).astype(BF16)

    gather_own(2)
    for copy in loads[2:]:
        copy.wait()
    for copy in weights:
        copy.wait_recv()
    near_end(0)
    near_end(1)
    products(0, 0)
    products(0, 1)
    gather_pass(2)
    products(0, 2)
    products(0, 3)
    gather_own(3)
    sum_first(0)
    gather_own(4)
    gather_pass(3)
    sum_second(0)
    gather_end(2)
    gather_end(3)
    products(1, 0)
    products(1, 1)
    gather_pass(4)
    products(1, 2)
    products(1, 3)
    gather_own(5)
    sum_first(1)
    sum_last(0)
    gather_own(6)
    gather_pass(5)
    sum_second(1)
    gather_end(4)
    gather_end(5)
    products(2, 0)
    products(2, 1)
    gather_own(7)
    gather_pass(6)
    products(2, 2)
    products(2, 3)
    sum_first(2)
    sum_last(1)
    gather_pass(7)
    partner_rows(0)
    partner_rows(1)
    weight_grads(0, 0, 0)
    sum_second(2)
    gather_end(6)
    weight_grads(0, 0, 1)
    gather_end(7)
    products(3, 0)
    products(3, 1)
    products(3, 2)
    products(3, 3)
    sum_first(3)
    sum_last(2)
    weight_grads(0, 1, 0)
    sum_second(3)
    weight_grads(0, 1, 1)
    partner_rows(2)
    partner_rows(3)
    weight_grads(1, 0, 0)
    sum_last(3)
    weight_grads(1, 0, 1)
    weight_grads(1, 1, 0)
    weight_grads(1, 1, 1)

    got = ret.at[pl.ds(1, NS - 1)]
    sent = res.at[pl.ds(1, NS - 1)]
    remote(sent, got, ret_send, ret_recv, left_dev).wait()
    sent = near.at[:, pl.ds(1, NEAR - 1)]
    remote(sent, sent, near_send, yz_recv.at[0], left_dev).wait_send()
    remote(far, far, far_send, yz_recv.at[0], left_dev).wait_send()
    for i in range(2):
        own = rows.at[0, pl.ds(NEAR, NS - NEAR)]
        half = rows.at[0, pl.ds(NEAR, (NS - NEAR) // 2)]
        remote(own, own, own_send.at[i], plus_recv.at[0], left_dev).wait_send()
        remote(half, half, fwd_send.at[i], plus_recv.at[0], left_dev).wait_send()
        weights[i].wait_send()
        remote(ra, ra, first_send.at[i], ra_recv.at[0], left_dev).wait_send()
        remote(rp, rp, second_send.at[i], rp_recv.at[0], left_dev).wait_send()
    remote(prows, prows, dp_send.at[0], prow_recv.at[0], other_dev).wait_send()
    remote(hs, phs, dp_send.at[1], phs_recv.at[0], other_dev).wait_send()


def finish(expert_hbm, slot_hbm, ret, gu, gd, gt_out, gu_out, gd_out, expert_ref, slot_ref, gt, sems):
    small = [
        pltpu.make_async_copy(expert_hbm, expert_ref, sems.at[5]),
        pltpu.make_async_copy(slot_hbm, slot_ref, sems.at[6]),
    ]
    stores = []
    for i in range(4):
        src, dst = ((gu, gu_out), (gd, gd_out))[i // 2]
        where = pl.ds(QUARTER * (i % 2), QUARTER)
        stores.append(pltpu.make_async_copy(src.at[where], dst.at[where], sems.at[i]))
    for copy in small + stores:
        copy.start()
    for copy in small:
        copy.wait()
    pos = positions(expert_ref[...], slot_ref[...])
    onehot = (lax.broadcasted_iota(jnp.int32, (NS * CAP, pos.shape[1]), 0) == pos).astype(BF16)
    gt[...] = dot(onehot, ret[...].reshape(NS * CAP, QUARTER), ((0,), (0,))).astype(BF16)
    stores.append(pltpu.make_async_copy(gt, gt_out, sems.at[4]))
    stores[4].start()
    for copy in stores:
        copy.wait()


def local(tokens, grad_output, gate_prob, expert_index, slot_index, up_weight, down_weight):
    count = tokens.shape[0]
    expert, slot, gate, tokens, grad_output, up, down = (
        pltpu.with_memory_space_constraint(a, pltpu.HBM)
        for a in (
            expert_index.reshape(1, count), slot_index.reshape(1, count), gate_prob.reshape(1, count),
            tokens, grad_output, up_weight[0], down_weight[0],
        )
    )
    vmem = pl.BlockSpec(memory_space=pltpu.VMEM)
    hbm = pl.BlockSpec(memory_space=pltpu.HBM)
    dma = pltpu.SemaphoreType.DMA
    shape = jax.ShapeDtypeStruct
    returned, grad_up, grad_down = pl.pallas_call(
        kernel,
        out_shape=(
            shape((NS, CAP, QUARTER), BF16),
            shape((1024, 1024), BF16),
            shape((1024, 1024), BF16),
        ),
        in_specs=[hbm] * 7,
        out_specs=(vmem, vmem, vmem),
        scratch_shapes=[
            pltpu.VMEM((1, count), jnp.int32),
            pltpu.VMEM((1, count), jnp.int32),
            pltpu.VMEM((1, count), F32),
            pltpu.VMEM((count, 2048), BF16),
            pltpu.VMEM((count, 2048), BF16),
            pltpu.VMEM((4, NEAR, 2, CAP, QUARTER), BF16),
            pltpu.VMEM((NS - NEAR, 2, CAP, QUARTER), BF16),
            pltpu.VMEM((4, NS, 2, CAP, QUARTER), BF16),
            pltpu.VMEM((2, NS, 2, CAP, QUARTER), BF16),
            pltpu.VMEM((2048, 1024), BF16),
            pltpu.VMEM((2048, 1024), BF16),
            pltpu.VMEM((2, 512, 1024), BF16),
            pltpu.VMEM((2, 512, 1024), BF16),
            pltpu.VMEM((PAIRS, 4, 128, QUARTER), BF16),
            pltpu.VMEM((PAIRS, 64, QUARTER), BF16),
            pltpu.VMEM((PAIRS, 64, QUARTER), BF16),
            pltpu.VMEM((PAIRS, 128, QUARTER), BF16),
            pltpu.VMEM((PAIRS, 128, QUARTER), BF16),
            pltpu.VMEM((NS, CAP, QUARTER), BF16),
            pltpu.VMEM((2, 1024, 1024), F32),
            dma((4,)), dma((3,)), dma, dma, dma((NZ,)), dma((2,)), dma((NZ,)), dma((NZ,)), dma((2,)), dma((NZ,)), dma((NZ,)),
            dma((2,)), dma((2,)), dma((2,)), dma((PAIRS,)), dma((PAIRS,)),
            dma((2,)), dma((PAIRS,)), dma((PAIRS,)), dma((2,)), dma((PAIRS,)), dma((PAIRS,)), dma, dma,
        ],
        compiler_params=pltpu.CompilerParams(
            collective_id=0, has_side_effects=True, vmem_limit_bytes=44 * 2**20
        ),
        cost_estimate=pl.CostEstimate(flops=11 * 10**9, bytes_accessed=12 * 2**20, transcendentals=2**19),
        name="expert_layer",
    )(expert, slot, gate, tokens, grad_output, up, down)
    grad_tokens, grad_up, grad_down = pl.pallas_call(
        finish,
        out_shape=(
            shape((count, QUARTER), BF16),
            shape((1024, 1024), BF16),
            shape((1024, 1024), BF16),
        ),
        in_specs=[hbm, hbm, vmem, vmem, vmem],
        out_specs=(hbm, hbm, hbm),
        scratch_shapes=[
            pltpu.VMEM((1, count), jnp.int32),
            pltpu.VMEM((1, count), jnp.int32),
            pltpu.VMEM((count, QUARTER), BF16),
            dma((7,)),
        ],
        compiler_params=pltpu.CompilerParams(vmem_limit_bytes=16 * 2**20),
        name="finish",
    )(expert, slot, returned, grad_up, grad_down)
    return grad_tokens, grad_up[None], grad_down[None]


def solution(mesh):
    placed = (
        P(("expert", "dp"), None),
        P(("expert", "dp"), None),
        P(("expert", "dp")),
        P(("expert", "dp"), None),
        P(("expert", "dp"), None),
        P("expert", "dp", "tensor"),
        P("expert", "dp", "tensor"),
    )
    return jax.shard_map(
        local,
        mesh=mesh,
        in_specs=placed,
        out_specs=(
            P(("expert", "dp"), "tensor"),
            P("expert", "dp", "tensor"),
            P("expert", "dp", "tensor"),
        ),
        check_vma=False,
    )
```

```python
import jax
import jax.numpy as jnp
from jax import lax
from jax.experimental import pallas as pl
from jax.experimental.pallas import tpu as pltpu
from jax.sharding import PartitionSpec as P

MESH = pl.DeviceIdType.MESH
F32 = jnp.float32
BF16 = jnp.bfloat16
ROOT = 0.7978845608028654
CUBE = 0.044715

NY, NZ, NX = 4, 8, 4
CAP = 16
NS = NY * NZ
QUARTER = 512
PAIRS = 4
OFFSETS = (
    (0, 0), (1, 0), (3, 0), (2, 0),
    (0, 1), (0, -1), (1, 1), (3, -1),
    (2, 1), (2, -1), (3, 1), (1, -1),
    (0, 2), (0, -2), (1, 2), (1, -2),
    (2, 2), (2, -2), (3, 2), (3, -2),
    (0, 3), (0, -3), (1, 3), (1, -3),
    (2, 3), (2, -3), (3, 3), (3, -3),
    (0, 4), (1, 4), (2, 4), (3, 4),
)
NEAR = 8
SEND_ORDER = (2, 0, 3, 4, 5, 6, 7, 1)


def positions(expert, slot):
    e = lax.axis_index("expert")
    y, z = e // NZ, e % NZ
    code = (((expert >> 3) - y) & (NY - 1)) * NZ + (((expert & (NZ - 1)) - z) & (NZ - 1))
    place = jnp.zeros_like(code)
    for s, (dy, dz) in enumerate(OFFSETS):
        place = place + jnp.where(code == dy * NZ + dz % NZ, s, 0)
    return place * CAP + slot


def dot(a, b, dims):
    return lax.dot_general(a, b, (dims, ((), ())), preferred_element_type=F32)


def activation(pre, back):
    square = pre * pre
    bent = jnp.tanh(ROOT * (pre + CUBE * (pre * square)))
    share = 0.5 * (1.0 + bent)
    slope = share + pre * (0.5 * (1.0 - bent * bent)) * (ROOT * (1.0 + 3.0 * CUBE * square))
    return (pre * share).astype(BF16), (back * slope).astype(BF16)


def kernel(
    expert_hbm, slot_hbm, gate_hbm, tok_hbm, gout_hbm, up_hbm, down_hbm,
    ret, gu, gd,
    expert_ref, slot_ref, gate_ref, tokv, goutv, near, far, rows, prows, up, down, hs, phs, inp, ra, rb, rp, rm, res, gsum,
    load_sem, small_sem, near_send, far_send, yz_recv, own_send, plus_recv, minus_recv, fwd_send, fplus_recv, fminus_recv,
    w_send, w_recv, dp_send, prow_recv, phs_recv,
    first_send, ra_recv, rb_recv, second_send, rp_recv, rm_recv, ret_send, ret_recv,
):
    t = lax.axis_index("tensor")
    e = lax.axis_index("expert")
    d = lax.axis_index("dp")
    y, z = e // NZ, e % NZ
    left, right, across = (t + 3) % NX, (t + 1) % NX, (t + 2) % NX
    other = 1 - d

    def at_offset(s, sign):
        dy, dz = OFFSETS[s]
        return (t, ((y + sign * dy + NY) % NY) * NZ + (z + sign * dz + NZ) % NZ, d)

    right_dev, left_dev, other_dev = (right, e, d), (left, e, d), (t, e, other)

    def remote(src, dst, send, recv, dev):
        return pltpu.make_async_remote_copy(
            src_ref=src, dst_ref=dst, send_sem=send, recv_sem=recv, device_id=dev, device_id_type=MESH
        )

    loads = [
        pltpu.make_async_copy(tok_hbm, tokv, load_sem.at[0]),
        pltpu.make_async_copy(gout_hbm, goutv, load_sem.at[1]),
        pltpu.make_async_copy(up_hbm, up.at[pl.ds(d * 1024, 1024)], load_sem.at[2]),
        pltpu.make_async_copy(down_hbm, down.at[pl.ds(d * 1024, 1024)], load_sem.at[3]),
    ]
    small = [
        pltpu.make_async_copy(src, dst, small_sem.at[i])
        for i, (src, dst) in enumerate(((expert_hbm, expert_ref), (slot_hbm, slot_ref), (gate_hbm, gate_ref)))
    ]
    for copy in small + loads[:2]:
        copy.start()

    barrier = pltpu.get_barrier_semaphore()

    for dev in (right_dev, left_dev, other_dev):
        pl.semaphore_signal(barrier, inc=1, device_id=dev, device_id_type=MESH)
    for s in range(1, NS):
        pl.semaphore_signal(barrier, inc=1, device_id=at_offset(s, 1), device_id_type=MESH)

    for copy in small:
        copy.wait()
    pos = positions(expert_ref[...], slot_ref[...])
    gate = gate_ref[...]
    hot_near = lax.broadcasted_iota(jnp.int32, (NEAR * CAP, pos.shape[1]), 0) == pos
    hot_far = lax.broadcasted_iota(jnp.int32, ((NS - NEAR) * CAP, pos.shape[1]), 0) + NEAR * CAP == pos
    gate_near = jnp.sum(jnp.where(hot_near, gate, 0.0), axis=1, keepdims=True)
    gate_far = jnp.sum(jnp.where(hot_far, gate, 0.0), axis=1, keepdims=True)
    hot_near = hot_near.astype(BF16)
    hot_far = hot_far.astype(BF16)
    mine = pl.ds(pl.multiple_of(t * QUARTER, QUARTER), QUARTER)
    for part, buf in ((0, tokv), (1, goutv)):
        loads[part].wait()
        placed = dot(hot_far, buf[:, mine], ((1,), (0,)))
        if part == 1:
            placed = placed * gate_far
        far[:, part] = placed.astype(BF16).reshape(NS - NEAR, CAP, QUARTER)
        for q in range(4):
            placed = dot(hot_near, buf[:, q * QUARTER:(q + 1) * QUARTER], ((1,), (0,)))
            if part == 1:
                placed = placed * gate_near
            placed = placed.astype(BF16).reshape(NEAR, CAP, QUARTER)
            near[q, :, part] = placed
            rows[q, 0, part] = placed[0]

    for copy in loads[2:]:
        copy.start()
    pl.semaphore_wait(barrier, NS - 1 + 3)

    for g in SEND_ORDER:
        for s in range(max(4 * g, 1), 4 * g + 4):
            if s < NEAR:
                remote(near.at[:, s], rows.at[:, s], near_send, yz_recv.at[g], at_offset(s, 1)).start()
            else:
                remote(far.at[s - NEAR], rows.at[t, s], far_send, yz_recv.at[g], at_offset(s, 1)).start()
    weights = []
    for i, (src, dst) in enumerate(((up_hbm, up), (down_hbm, down))):
        weights.append(remote(src, dst.at[pl.ds(d * 1024, 1024)], w_send.at[i], w_recv.at[i], other_dev))
        weights[i].start()

    def block(q, k, n=NY, skip=0):
        return rows.at[q, pl.ds(NY * k + skip, n)]

    def gather_own(k):
        mine = block(t, k)
        remote(mine, mine, far_send, yz_recv.at[k], left_dev).wait_recv()
        remote(mine, mine, own_send.at[0], plus_recv.at[k], right_dev).start()
        remote(mine, mine, own_send.at[1], minus_recv.at[k], left_dev).start()

    def gather_pass(k):
        got = block(left, k)
        remote(got, got, own_send.at[0], plus_recv.at[k], right_dev).wait_recv()
        half = block(left, k, 2)
        remote(half, half, fwd_send.at[0], fplus_recv.at[k], right_dev).start()
        got = block(right, k)
        remote(got, got, own_send.at[1], minus_recv.at[k], left_dev).wait_recv()
        half = block(right, k, 2, 2)
        remote(half, half, fwd_send.at[1], fminus_recv.at[k], left_dev).start()

    def gather_end(k):
        half = block(across, k, 2)
        remote(half, half, fwd_send.at[0], fplus_recv.at[k], right_dev).wait_recv()
        half = block(across, k, 2, 2)
        remote(half, half, fwd_send.at[1], fminus_recv.at[k], left_dev).wait_recv()

    def near_end(g):
        got = rows.at[:, pl.ds(max(4 * g, 1), 4 * g + 4 - max(4 * g, 1))]
        remote(got, got, near_send, yz_recv.at[g], left_dev).wait_recv()

    def products(p, c):
        part = pl.ds(8 * p, 8)
        span = pl.ds(128 * p, 128)
        if c == 0:
            remote(
                rows.at[pl.ds(2 * other, 2), part], prows.at[:, part], dp_send.at[0], prow_recv.at[p], other_dev
            ).start()
        cols = pl.ds(256 * c, 256)
        pre = jnp.zeros((128, 256), F32)
        back = jnp.zeros((128, 256), F32)
        for q in range(4):
            depth = pl.ds(q * QUARTER, QUARTER)
            pre += dot(rows[q, part, 0].reshape(128, QUARTER), up[depth, cols], ((1,), (0,)))
            back += dot(rows[q, part, 1].reshape(128, QUARTER), down[depth, cols], ((1,), (0,)))
        hidden, slope = activation(pre, back)
        hs[0, span, cols] = hidden
        hs[1, span, cols] = slope
        if c == 3:
            remote(hs.at[:, span], phs.at[:, span], dp_send.at[1], phs_recv.at[p], other_dev).start()

    def input_share(p, q):
        span = pl.ds(128 * p, 128)
        depth = pl.ds(pl.multiple_of(q * QUARTER, QUARTER), QUARTER)
        inp[p, q] = dot(hs[1, span, :], up[depth, :], ((1,), (1,))).astype(BF16)

    def sum_first(p):
        input_share(p, across)
        remote(
            inp.at[p, across, pl.ds(0, 64)], ra.at[p], first_send.at[0], ra_recv.at[p], right_dev
        ).start()
        remote(
            inp.at[p, across, pl.ds(64, 64)], rb.at[p], first_send.at[1], rb_recv.at[p], left_dev
        ).start()
        input_share(p, right)
        input_share(p, left)
        input_share(p, t)

    def sum_second(p):
        remote(ra.at[p], ra.at[p], first_send.at[0], ra_recv.at[p], right_dev).wait_recv()
        top = pl.ds(0, 64)
        inp[p, right, top] = (inp[p, right, top].astype(F32) + ra[p].astype(F32)).astype(BF16)
        remote(inp.at[p, right], rp.at[p], second_send.at[0], rp_recv.at[p], right_dev).start()
        remote(rb.at[p], rb.at[p], first_send.at[1], rb_recv.at[p], left_dev).wait_recv()
        low = pl.ds(64, 64)
        inp[p, left, low] = (inp[p, left, low].astype(F32) + rb[p].astype(F32)).astype(BF16)
        remote(inp.at[p, left], rm.at[p], second_send.at[1], rm_recv.at[p], left_dev).start()

    def sum_last(p):
        remote(rp.at[p], rp.at[p], second_send.at[0], rp_recv.at[p], right_dev).wait_recv()
        remote(rm.at[p], rm.at[p], second_send.at[1], rm_recv.at[p], left_dev).wait_recv()
        total = inp[p, t].astype(F32) + rp[p].astype(F32) + rm[p].astype(F32)
        res[pl.ds(8 * p, 8)] = total.astype(BF16).reshape(8, CAP, QUARTER)

        if p == 0:
            ret[0] = total[:CAP].astype(BF16)
        for s in range(max(8 * p, 1), 8 * p + 8):
            remote(res.at[s], ret.at[s], ret_send, ret_recv, at_offset(s, -1)).start()

    def partner_rows(p):
        part = pl.ds(8 * p, 8)
        span = pl.ds(128 * p, 128)
        remote(
            rows.at[pl.ds(0, 2), part], prows.at[:, part], dp_send.at[0], prow_recv.at[p], other_dev
        ).wait_recv()
        remote(hs.at[:, span], phs.at[:, span], dp_send.at[1], phs_recv.at[p], other_dev).wait_recv()

    def weight_grads(half, which, q):
        out = gu if which == 0 else gd
        where = pl.ds(q * QUARTER, QUARTER)
        factors = []
        for p in ((1, 2), (3, 0))[half]:
            part = pl.ds(8 * p, 8)
            span = pl.ds(128 * p, 128)
            factors.append((rows[2 * d + q, part, which].reshape(128, QUARTER), hs, span))
            factors.append((prows[q, part, which].reshape(128, QUARTER), phs, span))
        left_factor = jnp.concatenate([rows for rows, _, _ in factors], axis=0)
        for c in range(0, 1024, 256):
            cols = pl.ds(c, 256)
            right_factor = jnp.concatenate([ref[1 - which, span, cols] for _, ref, span in factors], axis=0)
            total = dot(left_factor, right_factor, ((0,), (0,)))
            if half == 0:
                gsum[which, where, cols] = total
            else:
                out[where, cols] = (gsum[which, where, cols] + total).astype(BF16)

    gather_own(2)
    gather_pass(2)
    for copy in loads[2:]:
        copy.wait()
    for copy in weights:
        copy.wait_recv()
    gather_own(3)
    gather_own(4)
    gather_pass(3)
    gather_pass(4)
    gather_end(2)
    gather_end(3)
    for c in range(4):
        products(1, c)
    gather_own(5)
    gather_own(6)
    sum_first(1)
    gather_pass(5)
    sum_second(1)
    gather_pass(6)
    gather_end(4)
    gather_end(5)
    products(2, 0)
    products(2, 1)
    gather_own(7)
    products(2, 2)
    products(2, 3)
    sum_first(2)
    sum_last(1)
    gather_pass(7)
    sum_second(2)
    partner_rows(1)
    partner_rows(2)
    weight_grads(0, 0, 0)
    gather_end(6)
    gather_end(7)
    for c in range(4):
        products(3, c)
    sum_first(3)
    sum_last(2)
    near_end(0)
    near_end(1)
    for c in range(4):
        products(0, c)
    sum_second(3)
    sum_first(0)
    weight_grads(0, 0, 1)
    weight_grads(0, 1, 0)
    sum_second(0)
    sum_last(3)
    weight_grads(0, 1, 1)
    partner_rows(3)
    partner_rows(0)
    weight_grads(1, 0, 0)
    sum_last(0)
    weight_grads(1, 0, 1)
    weight_grads(1, 1, 0)
    weight_grads(1, 1, 1)

    got = ret.at[pl.ds(1, NS - 1)]
    sent = res.at[pl.ds(1, NS - 1)]
    remote(sent, got, ret_send, ret_recv, left_dev).wait()
    sent = near.at[:, pl.ds(1, NEAR - 1)]
    remote(sent, sent, near_send, yz_recv.at[0], left_dev).wait_send()
    remote(far, far, far_send, yz_recv.at[0], left_dev).wait_send()
    for i in range(2):
        own = rows.at[0, pl.ds(NEAR, NS - NEAR)]
        half = rows.at[0, pl.ds(NEAR, (NS - NEAR) // 2)]
        remote(own, own, own_send.at[i], plus_recv.at[0], left_dev).wait_send()
        remote(half, half, fwd_send.at[i], plus_recv.at[0], left_dev).wait_send()
        weights[i].wait_send()
        remote(ra, ra, first_send.at[i], ra_recv.at[0], left_dev).wait_send()
        remote(rp, rp, second_send.at[i], rp_recv.at[0], left_dev).wait_send()
    remote(prows, prows, dp_send.at[0], prow_recv.at[0], other_dev).wait_send()
    remote(hs, phs, dp_send.at[1], phs_recv.at[0], other_dev).wait_send()


def finish(expert_hbm, slot_hbm, ret, gu, gd, gt_out, gu_out, gd_out, expert_ref, slot_ref, gt, sems):
    small = [
        pltpu.make_async_copy(expert_hbm, expert_ref, sems.at[5]),
        pltpu.make_async_copy(slot_hbm, slot_ref, sems.at[6]),
    ]
    stores = []
    for i in range(4):
        src, dst = ((gu, gu_out), (gd, gd_out))[i // 2]
        where = pl.ds(QUARTER * (i % 2), QUARTER)
        stores.append(pltpu.make_async_copy(src.at[where], dst.at[where], sems.at[i]))
    for copy in small + stores:
        copy.start()
    for copy in small:
        copy.wait()
    pos = positions(expert_ref[...], slot_ref[...])
    onehot = (lax.broadcasted_iota(jnp.int32, (NS * CAP, pos.shape[1]), 0) == pos).astype(BF16)
    gt[...] = dot(onehot, ret[...].reshape(NS * CAP, QUARTER), ((0,), (0,))).astype(BF16)
    stores.append(pltpu.make_async_copy(gt, gt_out, sems.at[4]))
    stores[4].start()
    for copy in stores:
        copy.wait()


def local(tokens, grad_output, gate_prob, expert_index, slot_index, up_weight, down_weight):
    count = tokens.shape[0]
    expert, slot, gate, tokens, grad_output, up, down = (
        pltpu.with_memory_space_constraint(a, pltpu.HBM)
        for a in (
            expert_index.reshape(1, count), slot_index.reshape(1, count), gate_prob.reshape(1, count),
            tokens, grad_output, up_weight[0], down_weight[0],
        )
    )
    vmem = pl.BlockSpec(memory_space=pltpu.VMEM)
    hbm = pl.BlockSpec(memory_space=pltpu.HBM)
    dma = pltpu.SemaphoreType.DMA
    shape = jax.ShapeDtypeStruct
    returned, grad_up, grad_down = pl.pallas_call(
        kernel,
        out_shape=(
            shape((NS, CAP, QUARTER), BF16),
            shape((1024, 1024), BF16),
            shape((1024, 1024), BF16),
        ),
        in_specs=[hbm] * 7,
        out_specs=(vmem, vmem, vmem),
        scratch_shapes=[
            pltpu.VMEM((1, count), jnp.int32),
            pltpu.VMEM((1, count), jnp.int32),
            pltpu.VMEM((1, count), F32),
            pltpu.VMEM((count, 2048), BF16),
            pltpu.VMEM((count, 2048), BF16),
            pltpu.VMEM((4, NEAR, 2, CAP, QUARTER), BF16),
            pltpu.VMEM((NS - NEAR, 2, CAP, QUARTER), BF16),
            pltpu.VMEM((4, NS, 2, CAP, QUARTER), BF16),
            pltpu.VMEM((2, NS, 2, CAP, QUARTER), BF16),
            pltpu.VMEM((2048, 1024), BF16),
            pltpu.VMEM((2048, 1024), BF16),
            pltpu.VMEM((2, 512, 1024), BF16),
            pltpu.VMEM((2, 512, 1024), BF16),
            pltpu.VMEM((PAIRS, 4, 128, QUARTER), BF16),
            pltpu.VMEM((PAIRS, 64, QUARTER), BF16),
            pltpu.VMEM((PAIRS, 64, QUARTER), BF16),
            pltpu.VMEM((PAIRS, 128, QUARTER), BF16),
            pltpu.VMEM((PAIRS, 128, QUARTER), BF16),
            pltpu.VMEM((NS, CAP, QUARTER), BF16),
            pltpu.VMEM((2, 1024, 1024), F32),
            dma((4,)), dma((3,)), dma, dma, dma((NZ,)), dma((2,)), dma((NZ,)), dma((NZ,)), dma((2,)), dma((NZ,)), dma((NZ,)),
            dma((2,)), dma((2,)), dma((2,)), dma((PAIRS,)), dma((PAIRS,)),
            dma((2,)), dma((PAIRS,)), dma((PAIRS,)), dma((2,)), dma((PAIRS,)), dma((PAIRS,)), dma, dma,
        ],
        compiler_params=pltpu.CompilerParams(
            collective_id=0, has_side_effects=True, vmem_limit_bytes=44 * 2**20
        ),
        cost_estimate=pl.CostEstimate(flops=11 * 10**9, bytes_accessed=12 * 2**20, transcendentals=2**19),
        name="expert_layer",
    )(expert, slot, gate, tokens, grad_output, up, down)
    grad_tokens, grad_up, grad_down = pl.pallas_call(
        finish,
        out_shape=(
            shape((count, QUARTER), BF16),
            shape((1024, 1024), BF16),
            shape((1024, 1024), BF16),
        ),
        in_specs=[hbm, hbm, vmem, vmem, vmem],
        out_specs=(hbm, hbm, hbm),
        scratch_shapes=[
            pltpu.VMEM((1, count), jnp.int32),
            pltpu.VMEM((1, count), jnp.int32),
            pltpu.VMEM((count, QUARTER), BF16),
            dma((7,)),
        ],
        compiler_params=pltpu.CompilerParams(vmem_limit_bytes=16 * 2**20),
        name="finish",
    )(expert, slot, returned, grad_up, grad_down)
    return grad_tokens, grad_up[None], grad_down[None]


def solution(mesh):
    placed = (
        P(("expert", "dp"), None),
        P(("expert", "dp"), None),
        P(("expert", "dp")),
        P(("expert", "dp"), None),
        P(("expert", "dp"), None),
        P("expert", "dp", "tensor"),
        P("expert", "dp", "tensor"),
    )
    return jax.shard_map(
        local,
        mesh=mesh,
        in_specs=placed,
        out_specs=(
            P(("expert", "dp"), "tensor"),
            P("expert", "dp", "tensor"),
            P("expert", "dp", "tensor"),
        ),
        check_vma=False,
    )
```

```python
import jax
import jax.numpy as jnp
from jax import lax
from jax.experimental import pallas as pl
from jax.experimental.pallas import tpu as pltpu
from jax.sharding import PartitionSpec as P

MESH = pl.DeviceIdType.MESH
F32 = jnp.float32
BF16 = jnp.bfloat16
ROOT = 0.7978845608028654
CUBE = 0.044715

NY, NZ, NX = 4, 8, 4
CAP = 16
NS = NY * NZ
QUARTER = 512
PAIRS = 4
OFFSETS = (
    (0, 0), (1, 0), (3, 0), (2, 0),
    (0, 1), (0, -1), (1, 1), (3, -1),
    (2, 1), (2, -1), (3, 1), (1, -1),
    (0, 2), (0, -2), (1, 2), (1, -2),
    (2, 2), (2, -2), (3, 2), (3, -2),
    (0, 3), (0, -3), (1, 3), (1, -3),
    (2, 3), (2, -3), (3, 3), (3, -3),
    (0, 4), (1, 4), (2, 4), (3, 4),
)
NEAR = 8
SEND_ORDER = (2, 0, 3, 4, 5, 6, 7, 1)


def positions(expert, slot):
    e = lax.axis_index("expert")
    y, z = e // NZ, e % NZ
    code = (((expert >> 3) - y) & (NY - 1)) * NZ + (((expert & (NZ - 1)) - z) & (NZ - 1))
    place = jnp.zeros_like(code)
    for s, (dy, dz) in enumerate(OFFSETS):
        place = place + jnp.where(code == dy * NZ + dz % NZ, s, 0)
    return place * CAP + slot


def dot(a, b, dims):
    return lax.dot_general(a, b, (dims, ((), ())), preferred_element_type=F32)


def activation(pre, back):
    square = pre * pre
    bent = jnp.tanh(ROOT * (pre + CUBE * (pre * square)))
    share = 0.5 * (1.0 + bent)
    slope = share + pre * (0.5 * (1.0 - bent * bent)) * (ROOT * (1.0 + 3.0 * CUBE * square))
    return (pre * share).astype(BF16), (back * slope).astype(BF16)


def kernel(
    expert_hbm, slot_hbm, gate_hbm, tok_hbm, gout_hbm, up_hbm, down_hbm,
    ret, gu, gd,
    expert_ref, slot_ref, gate_ref, tokv, goutv, near, far, rows, prows, up, down, hs, phs, inp, ra, rb, rp, rm, res, gsum,
    load_sem, small_sem, near_send, far_send, yz_recv, own_send, plus_recv, minus_recv, fwd_send, fplus_recv, fminus_recv,
    w_send, w_recv, dp_send, prow_recv, phs_recv,
    first_send, ra_recv, rb_recv, second_send, rp_recv, rm_recv, ret_send, ret_recv,
):
    t = lax.axis_index("tensor")
    e = lax.axis_index("expert")
    d = lax.axis_index("dp")
    y, z = e // NZ, e % NZ
    left, right, across = (t + 3) % NX, (t + 1) % NX, (t + 2) % NX
    other = 1 - d

    def at_offset(s, sign):
        dy, dz = OFFSETS[s]
        return (t, ((y + sign * dy + NY) % NY) * NZ + (z + sign * dz + NZ) % NZ, d)

    right_dev, left_dev, other_dev = (right, e, d), (left, e, d), (t, e, other)

    def remote(src, dst, send, recv, dev):
        return pltpu.make_async_remote_copy(
            src_ref=src, dst_ref=dst, send_sem=send, recv_sem=recv, device_id=dev, device_id_type=MESH
        )

    loads = [
        pltpu.make_async_copy(tok_hbm, tokv, load_sem.at[0]),
        pltpu.make_async_copy(gout_hbm, goutv, load_sem.at[1]),
        pltpu.make_async_copy(up_hbm, up.at[pl.ds(d * 1024, 1024)], load_sem.at[2]),
        pltpu.make_async_copy(down_hbm, down.at[pl.ds(d * 1024, 1024)], load_sem.at[3]),
    ]
    small = [
        pltpu.make_async_copy(src, dst, small_sem.at[i])
        for i, (src, dst) in enumerate(((expert_hbm, expert_ref), (slot_hbm, slot_ref), (gate_hbm, gate_ref)))
    ]
    for copy in small + loads[:2]:
        copy.start()

    barrier = pltpu.get_barrier_semaphore()

    for dev in (right_dev, left_dev, other_dev):
        pl.semaphore_signal(barrier, inc=1, device_id=dev, device_id_type=MESH)
    for s in range(1, NS):
        pl.semaphore_signal(barrier, inc=1, device_id=at_offset(s, 1), device_id_type=MESH)

    for copy in small:
        copy.wait()
    pos = positions(expert_ref[...], slot_ref[...])
    gate = gate_ref[...]
    hot_near = lax.broadcasted_iota(jnp.int32, (NEAR * CAP, pos.shape[1]), 0) == pos
    hot_far = lax.broadcasted_iota(jnp.int32, ((NS - NEAR) * CAP, pos.shape[1]), 0) + NEAR * CAP == pos
    gate_near = jnp.sum(jnp.where(hot_near, gate, 0.0), axis=1, keepdims=True)
    gate_far = jnp.sum(jnp.where(hot_far, gate, 0.0), axis=1, keepdims=True)
    hot_near = hot_near.astype(BF16)
    hot_far = hot_far.astype(BF16)
    mine = pl.ds(pl.multiple_of(t * QUARTER, QUARTER), QUARTER)
    for part, buf in ((0, tokv), (1, goutv)):
        loads[part].wait()
        placed = dot(hot_far, buf[:, mine], ((1,), (0,)))
        if part == 1:
            placed = placed * gate_far
        far[:, part] = placed.astype(BF16).reshape(NS - NEAR, CAP, QUARTER)
        for q in range(4):
            placed = dot(hot_near, buf[:, q * QUARTER:(q + 1) * QUARTER], ((1,), (0,)))
            if part == 1:
                placed = placed * gate_near
            placed = placed.astype(BF16).reshape(NEAR, CAP, QUARTER)
            near[q, :, part] = placed
            rows[q, 0, part] = placed[0]

    for copy in loads[2:]:
        copy.start()
    pl.semaphore_wait(barrier, NS - 1 + 3)

    for g in SEND_ORDER:
        for s in range(max(4 * g, 1), 4 * g + 4):
            if s < NEAR:
                remote(near.at[:, s], rows.at[:, s], near_send, yz_recv.at[g], at_offset(s, 1)).start()
            else:
                remote(far.at[s - NEAR], rows.at[t, s], far_send, yz_recv.at[g], at_offset(s, 1)).start()
    weights = []
    for i, (src, dst) in enumerate(((up_hbm, up), (down_hbm, down))):
        weights.append(remote(src, dst.at[pl.ds(d * 1024, 1024)], w_send.at[i], w_recv.at[i], other_dev))
        weights[i].start()

    def block(q, k, n=NY, skip=0):
        return rows.at[q, pl.ds(NY * k + skip, n)]

    def gather_own(k):
        mine = block(t, k)
        remote(mine, mine, far_send, yz_recv.at[k], left_dev).wait_recv()
        remote(mine, mine, own_send.at[0], plus_recv.at[k], right_dev).start()
        remote(mine, mine, own_send.at[1], minus_recv.at[k], left_dev).start()

    def gather_pass(k):
        got = block(left, k)
        remote(got, got, own_send.at[0], plus_recv.at[k], right_dev).wait_recv()
        half = block(left, k, 2)
        remote(half, half, fwd_send.at[0], fplus_recv.at[k], right_dev).start()
        got = block(right, k)
        remote(got, got, own_send.at[1], minus_recv.at[k], left_dev).wait_recv()
        half = block(right, k, 2, 2)
        remote(half, half, fwd_send.at[1], fminus_recv.at[k], left_dev).start()

    def gather_end(k):
        half = block(across, k, 2)
        remote(half, half, fwd_send.at[0], fplus_recv.at[k], right_dev).wait_recv()
        half = block(across, k, 2, 2)
        remote(half, half, fwd_send.at[1], fminus_recv.at[k], left_dev).wait_recv()

    def near_end(g):
        got = rows.at[:, pl.ds(max(4 * g, 1), 4 * g + 4 - max(4 * g, 1))]
        remote(got, got, near_send, yz_recv.at[g], left_dev).wait_recv()

    def products(p, c):
        part = pl.ds(8 * p, 8)
        span = pl.ds(128 * p, 128)
        if c == 0:
            remote(
                rows.at[pl.ds(2 * other, 2), part], prows.at[:, part], dp_send.at[0], prow_recv.at[p], other_dev
            ).start()
        cols = pl.ds(256 * c, 256)
        pre = jnp.zeros((128, 256), F32)
        back = jnp.zeros((128, 256), F32)
        for q in range(4):
            depth = pl.ds(q * QUARTER, QUARTER)
            pre += dot(rows[q, part, 0].reshape(128, QUARTER), up[depth, cols], ((1,), (0,)))
            back += dot(rows[q, part, 1].reshape(128, QUARTER), down[depth, cols], ((1,), (0,)))
        hidden, slope = activation(pre, back)
        hs[0, span, cols] = hidden
        hs[1, span, cols] = slope
        if c == 3:
            remote(hs.at[:, span], phs.at[:, span], dp_send.at[1], phs_recv.at[p], other_dev).start()

    def input_share(p, q):
        span = pl.ds(128 * p, 128)
        depth = pl.ds(pl.multiple_of(q * QUARTER, QUARTER), QUARTER)
        inp[p, q] = dot(hs[1, span, :], up[depth, :], ((1,), (1,))).astype(BF16)

    def sum_first(p):
        input_share(p, across)
        remote(
            inp.at[p, across, pl.ds(0, 64)], ra.at[p], first_send.at[0], ra_recv.at[p], right_dev
        ).start()
        remote(
            inp.at[p, across, pl.ds(64, 64)], rb.at[p], first_send.at[1], rb_recv.at[p], left_dev
        ).start()

    def sum_rest(p):
        input_share(p, right)
        input_share(p, left)
        input_share(p, t)

    def sum_second(p):
        remote(ra.at[p], ra.at[p], first_send.at[0], ra_recv.at[p], right_dev).wait_recv()
        top = pl.ds(0, 64)
        inp[p, right, top] = (inp[p, right, top].astype(F32) + ra[p].astype(F32)).astype(BF16)
        remote(inp.at[p, right], rp.at[p], second_send.at[0], rp_recv.at[p], right_dev).start()
        remote(rb.at[p], rb.at[p], first_send.at[1], rb_recv.at[p], left_dev).wait_recv()
        low = pl.ds(64, 64)
        inp[p, left, low] = (inp[p, left, low].astype(F32) + rb[p].astype(F32)).astype(BF16)
        remote(inp.at[p, left], rm.at[p], second_send.at[1], rm_recv.at[p], left_dev).start()

    def sum_last(p):
        remote(rp.at[p], rp.at[p], second_send.at[0], rp_recv.at[p], right_dev).wait_recv()
        remote(rm.at[p], rm.at[p], second_send.at[1], rm_recv.at[p], left_dev).wait_recv()
        total = inp[p, t].astype(F32) + rp[p].astype(F32) + rm[p].astype(F32)
        res[pl.ds(8 * p, 8)] = total.astype(BF16).reshape(8, CAP, QUARTER)

        if p == 0:
            ret[0] = total[:CAP].astype(BF16)
        for s in range(max(8 * p, 1), 8 * p + 8):
            remote(res.at[s], ret.at[s], ret_send, ret_recv, at_offset(s, -1)).start()

    def partner_rows(p):
        part = pl.ds(8 * p, 8)
        span = pl.ds(128 * p, 128)
        remote(
            rows.at[pl.ds(0, 2), part], prows.at[:, part], dp_send.at[0], prow_recv.at[p], other_dev
        ).wait_recv()
        remote(hs.at[:, span], phs.at[:, span], dp_send.at[1], phs_recv.at[p], other_dev).wait_recv()

    def weight_grads(half, which, q):
        out = gu if which == 0 else gd
        where = pl.ds(q * QUARTER, QUARTER)
        factors = []
        for p in ((1, 2), (3, 0))[half]:
            part = pl.ds(8 * p, 8)
            span = pl.ds(128 * p, 128)
            factors.append((rows[2 * d + q, part, which].reshape(128, QUARTER), hs, span))
            factors.append((prows[q, part, which].reshape(128, QUARTER), phs, span))
        left_factor = jnp.concatenate([rows for rows, _, _ in factors], axis=0)
        for c in range(0, 1024, 256):
            cols = pl.ds(c, 256)
            right_factor = jnp.concatenate([ref[1 - which, span, cols] for _, ref, span in factors], axis=0)
            total = dot(left_factor, right_factor, ((0,), (0,)))
            if half == 0:
                gsum[which, where, cols] = total
            else:
                out[where, cols] = (gsum[which, where, cols] + total).astype(BF16)

    gather_own(2)
    gather_pass(2)
    for copy in loads[2:]:
        copy.wait()
    for copy in weights:
        copy.wait_recv()
    gather_own(3)
    gather_own(4)
    gather_pass(3)
    gather_pass(4)
    gather_end(2)
    gather_end(3)
    for c in range(4):
        products(1, c)
    gather_own(5)
    gather_own(6)
    sum_first(1)
    gather_pass(5)
    sum_rest(1)
    sum_second(1)
    gather_pass(6)
    gather_end(4)
    gather_end(5)
    products(2, 0)
    products(2, 1)
    gather_own(7)
    products(2, 2)
    products(2, 3)
    sum_first(2)
    gather_pass(7)
    sum_rest(2)
    sum_last(1)
    sum_second(2)
    partner_rows(1)
    partner_rows(2)
    weight_grads(0, 0, 0)
    gather_end(6)
    gather_end(7)
    for c in range(4):
        products(3, c)
    sum_first(3)
    sum_rest(3)
    sum_last(2)
    near_end(0)
    near_end(1)
    products(0, 0)
    products(0, 1)
    sum_second(3)
    products(0, 2)
    products(0, 3)
    sum_first(0)
    sum_rest(0)
    weight_grads(0, 0, 1)
    weight_grads(0, 1, 0)
    sum_second(0)
    sum_last(3)
    weight_grads(0, 1, 1)
    partner_rows(3)
    partner_rows(0)
    weight_grads(1, 0, 0)
    sum_last(0)
    weight_grads(1, 0, 1)
    weight_grads(1, 1, 0)
    weight_grads(1, 1, 1)

    got = ret.at[pl.ds(1, NS - 1)]
    sent = res.at[pl.ds(1, NS - 1)]
    remote(sent, got, ret_send, ret_recv, left_dev).wait()
    sent = near.at[:, pl.ds(1, NEAR - 1)]
    remote(sent, sent, near_send, yz_recv.at[0], left_dev).wait_send()
    remote(far, far, far_send, yz_recv.at[0], left_dev).wait_send()
    for i in range(2):
        own = rows.at[0, pl.ds(NEAR, NS - NEAR)]
        half = rows.at[0, pl.ds(NEAR, (NS - NEAR) // 2)]
        remote(own, own, own_send.at[i], plus_recv.at[0], left_dev).wait_send()
        remote(half, half, fwd_send.at[i], plus_recv.at[0], left_dev).wait_send()
        weights[i].wait_send()
        remote(ra, ra, first_send.at[i], ra_recv.at[0], left_dev).wait_send()
        remote(rp, rp, second_send.at[i], rp_recv.at[0], left_dev).wait_send()
    remote(prows, prows, dp_send.at[0], prow_recv.at[0], other_dev).wait_send()
    remote(hs, phs, dp_send.at[1], phs_recv.at[0], other_dev).wait_send()


def finish(expert_hbm, slot_hbm, ret, gu, gd, gt_out, gu_out, gd_out, expert_ref, slot_ref, gt, sems):
    small = [
        pltpu.make_async_copy(expert_hbm, expert_ref, sems.at[5]),
        pltpu.make_async_copy(slot_hbm, slot_ref, sems.at[6]),
    ]
    stores = []
    for i in range(4):
        src, dst = ((gu, gu_out), (gd, gd_out))[i // 2]
        where = pl.ds(QUARTER * (i % 2), QUARTER)
        stores.append(pltpu.make_async_copy(src.at[where], dst.at[where], sems.at[i]))
    for copy in small + stores:
        copy.start()
    for copy in small:
        copy.wait()
    pos = positions(expert_ref[...], slot_ref[...])
    onehot = (lax.broadcasted_iota(jnp.int32, (NS * CAP, pos.shape[1]), 0) == pos).astype(BF16)
    gt[...] = dot(onehot, ret[...].reshape(NS * CAP, QUARTER), ((0,), (0,))).astype(BF16)
    stores.append(pltpu.make_async_copy(gt, gt_out, sems.at[4]))
    stores[4].start()
    for copy in stores:
        copy.wait()


def local(tokens, grad_output, gate_prob, expert_index, slot_index, up_weight, down_weight):
    count = tokens.shape[0]
    expert, slot, gate, tokens, grad_output, up, down = (
        pltpu.with_memory_space_constraint(a, pltpu.HBM)
        for a in (
            expert_index.reshape(1, count), slot_index.reshape(1, count), gate_prob.reshape(1, count),
            tokens, grad_output, up_weight[0], down_weight[0],
        )
    )
    vmem = pl.BlockSpec(memory_space=pltpu.VMEM)
    hbm = pl.BlockSpec(memory_space=pltpu.HBM)
    dma = pltpu.SemaphoreType.DMA
    shape = jax.ShapeDtypeStruct
    returned, grad_up, grad_down = pl.pallas_call(
        kernel,
        out_shape=(
            shape((NS, CAP, QUARTER), BF16),
            shape((1024, 1024), BF16),
            shape((1024, 1024), BF16),
        ),
        in_specs=[hbm] * 7,
        out_specs=(vmem, vmem, vmem),
        scratch_shapes=[
            pltpu.VMEM((1, count), jnp.int32),
            pltpu.VMEM((1, count), jnp.int32),
            pltpu.VMEM((1, count), F32),
            pltpu.VMEM((count, 2048), BF16),
            pltpu.VMEM((count, 2048), BF16),
            pltpu.VMEM((4, NEAR, 2, CAP, QUARTER), BF16),
            pltpu.VMEM((NS - NEAR, 2, CAP, QUARTER), BF16),
            pltpu.VMEM((4, NS, 2, CAP, QUARTER), BF16),
            pltpu.VMEM((2, NS, 2, CAP, QUARTER), BF16),
            pltpu.VMEM((2048, 1024), BF16),
            pltpu.VMEM((2048, 1024), BF16),
            pltpu.VMEM((2, 512, 1024), BF16),
            pltpu.VMEM((2, 512, 1024), BF16),
            pltpu.VMEM((PAIRS, 4, 128, QUARTER), BF16),
            pltpu.VMEM((PAIRS, 64, QUARTER), BF16),
            pltpu.VMEM((PAIRS, 64, QUARTER), BF16),
            pltpu.VMEM((PAIRS, 128, QUARTER), BF16),
            pltpu.VMEM((PAIRS, 128, QUARTER), BF16),
            pltpu.VMEM((NS, CAP, QUARTER), BF16),
            pltpu.VMEM((2, 1024, 1024), F32),
            dma((4,)), dma((3,)), dma, dma, dma((NZ,)), dma((2,)), dma((NZ,)), dma((NZ,)), dma((2,)), dma((NZ,)), dma((NZ,)),
            dma((2,)), dma((2,)), dma((2,)), dma((PAIRS,)), dma((PAIRS,)),
            dma((2,)), dma((PAIRS,)), dma((PAIRS,)), dma((2,)), dma((PAIRS,)), dma((PAIRS,)), dma, dma,
        ],
        compiler_params=pltpu.CompilerParams(
            collective_id=0, has_side_effects=True, vmem_limit_bytes=44 * 2**20
        ),
        cost_estimate=pl.CostEstimate(flops=11 * 10**9, bytes_accessed=12 * 2**20, transcendentals=2**19),
        name="expert_layer",
    )(expert, slot, gate, tokens, grad_output, up, down)
    grad_tokens, grad_up, grad_down = pl.pallas_call(
        finish,
        out_shape=(
            shape((count, QUARTER), BF16),
            shape((1024, 1024), BF16),
            shape((1024, 1024), BF16),
        ),
        in_specs=[hbm, hbm, vmem, vmem, vmem],
        out_specs=(hbm, hbm, hbm),
        scratch_shapes=[
            pltpu.VMEM((1, count), jnp.int32),
            pltpu.VMEM((1, count), jnp.int32),
            pltpu.VMEM((count, QUARTER), BF16),
            dma((7,)),
        ],
        compiler_params=pltpu.CompilerParams(vmem_limit_bytes=16 * 2**20),
        name="finish",
    )(expert, slot, returned, grad_up, grad_down)
    return grad_tokens, grad_up[None], grad_down[None]


def solution(mesh):
    placed = (
        P(("expert", "dp"), None),
        P(("expert", "dp"), None),
        P(("expert", "dp")),
        P(("expert", "dp"), None),
        P(("expert", "dp"), None),
        P("expert", "dp", "tensor"),
        P("expert", "dp", "tensor"),
    )
    return jax.shard_map(
        local,
        mesh=mesh,
        in_specs=placed,
        out_specs=(
            P(("expert", "dp"), "tensor"),
            P("expert", "dp", "tensor"),
            P("expert", "dp", "tensor"),
        ),
        check_vma=False,
    )
```
